32 devices in a mesh: groups: 2 (over x), expert: 8 (over z, y), latent: 2 (over core).
Axes of the slice: x: 2, y: 2, z: 4, core: 2. Of those that a mesh axis runs over, the one named last changes fastest.
Arguments:
- tokens: bfloat16 [8192, 4096], P(('groups', 'expert', 'latent')), parts along dimension 0, may hold values from -6 to 6
- routes: int32 [8192, 1], P(('groups', 'expert', 'latent')), parts along dimension 0, may hold values from 0 to 63; in each aligned block of 256 rows (0 to 255, 256 to 511, ...) at most 8 rows name the same one
- encoder: bfloat16 [128, 32, 4096], P(('groups', 'expert', 'latent')), parts along dimension 0, may hold values from -0.09375 to 0.09375
- encoder_bias: float32 [128, 32], P(('groups', 'expert', 'latent')), parts along dimension 0, may hold values from -3 to 3
- decoder: bfloat16 [128, 32, 4096], P(('groups', 'expert', 'latent')), parts along dimension 0, may hold values from -1 to 1
- encoder_mean: float32 [128, 32, 4096], P(('groups', 'expert', 'latent')), parts along dimension 0, may hold values from -256 to 256
- encoder_second: float32 [128, 32, 4096], P(('groups', 'expert', 'latent')), parts along dimension 0, may hold values from 16384 to 1638400
- bias_mean: float32 [128, 32], P(('groups', 'expert', 'latent')), parts along dimension 0, may hold values from -256 to 256
- bias_second: float32 [128, 32], P(('groups', 'expert', 'latent')), parts along dimension 0, may hold values from 16384 to 1638400
- decoder_mean: float32 [128, 32, 4096], P(('groups', 'expert', 'latent')), parts along dimension 0, may hold values from -18 to 18
- decoder_second: float32 [128, 32, 4096], P(('groups', 'expert', 'latent')), parts along dimension 0, may hold values from 4 to 400
Outputs:
- new_encoder: bfloat16 [128, 32, 4096], P(('groups', 'expert', 'latent')), parts along dimension 0
- new_encoder_bias: float32 [128, 32], P(('groups', 'expert', 'latent')), parts along dimension 0
- new_decoder: bfloat16 [128, 32, 4096], P(('groups', 'expert', 'latent')), parts along dimension 0
- new_encoder_mean: float32 [128, 32, 4096], P(('groups', 'expert', 'latent')), parts along dimension 0
- new_encoder_second: float32 [128, 32, 4096], P(('groups', 'expert', 'latent')), parts along dimension 0
- new_bias_mean: float32 [128, 32], P(('groups', 'expert', 'latent')), parts along dimension 0
- new_bias_second: float32 [128, 32], P(('groups', 'expert', 'latent')), parts along dimension 0
- new_decoder_mean: float32 [128, 32, 4096], P(('groups', 'expert', 'latent')), parts along dimension 0
- new_decoder_second: float32 [128, 32, 4096], P(('groups', 'expert', 'latent')), parts along dimension 0
- reconstruction: bfloat16 [8192, 4096], P(('groups', 'expert', 'latent')), parts along dimension 0
The draws below stay inside these ranges and needn't reach their ends.
There are 2 independent parts, one for each index of `groups`. The reference program is written for one: setup_inputs(seed, part) draws one part's arguments, and reference() takes and returns one part's arrays. A program takes and returns all parts, laid end to end along the dimension named above; each array names one. Nothing has to cross between parts.
Inputs may be any that keep to these rules, and one draw needn't show every extreme that they name: `routes`: among the 256 rows of one device (aligned blocks of 256 rows), no expert is named by more than 8 rows, a bound that some block reaches.
All inputs are finite; a program needn't handle non-finite values.
Results may differ from the reference program's by a relative error of at most 0.0049.
Values may be sent and summed in bfloat16 or wider, within the bound.
A program may use at most 128 MiB of HBM per device.

```python
import math
import jax
import jax.numpy as jnp
import numpy as np
from jax import lax

D = 4096
LAT_EXP = 32
TOK_DEV = 256
EXPERTS = 64
TOKENS = 4096
CAP = 8


def shard_levels(rng, dims, cuts, low, largest):
    def one(dim, blocks):
        steps = jax.random.uniform(jax.random.fold_in(jax.random.fold_in(rng, 6), dim), (blocks,), jnp.float32, low / len(cuts), largest / len(cuts))
        return jnp.repeat(jnp.exp(steps), dims[dim] // blocks).reshape((-1,) + (1,) * (len(dims) - dim - 1))

    gain = one(*cuts[0])
    for cut in cuts[1:]:
        gain = gain * one(*cut)
    return gain


def deal_out(key, own, number, rows, amount, top, limit, lean):
    ranking = jax.random.permutation(key, amount)
    crowded, common = load_shares(amount, rows * top, limit, lean, True), load_shares(amount, rows * top, limit, lean, False)
    places = jnp.arange(amount)

    def named(tallies, turn):
        used = int((tallies > 0).sum())
        fixed = max(1, used // 4)
        shifted = fixed + (places - fixed + turn * (used - fixed)) % max(1, amount - fixed)
        return jnp.zeros((amount,), jnp.int32).at[ranking[jnp.where(places < fixed, places, shifted)]].set(jnp.asarray(tallies, jnp.int32))

    tallies = jnp.where(number % 4 == 0, named(crowded, number // 4), named(common, number - number // 4 - 1))
    mixed = jax.random.permutation(jax.random.fold_in(own, 3), amount)
    donor, sink = mixed[0:amount // 2 * 2:2], mixed[1:amount // 2 * 2:2]
    room = jnp.minimum(tallies[donor] - 1, limit - tallies[sink]) // 2
    room = jnp.where((donor == ranking[0]) | (sink == ranking[0]) | (tallies[sink] == 0), 0, jnp.maximum(room, 0))
    shifted = jax.random.randint(jax.random.fold_in(own, 4), (amount // 2,), 0, 1 << 20) % (room + 1)
    tallies = tallies.at[donor].add(-shifted).at[sink].add(shifted)
    items = jnp.searchsorted(jnp.cumsum(tallies), jnp.arange(rows * top), side="right").astype(jnp.int32)
    table = items.reshape(top, rows).T
    table = table[jax.random.permutation(jax.random.fold_in(own, 1), rows)]
    turn = jax.random.randint(jax.random.fold_in(own, 2), (rows, 1), 0, top)
    return jnp.take_along_axis(table, (jnp.arange(top)[None, :] + turn) % top, axis=1)


def load_shares(amount, total, reach, skew, full):
    weights = [(1 << 20) // math.isqrt(rank ** skew) + 1 for rank in range(1, amount + 1)]
    largest = reach if full else min(reach, max(-(-total // amount), total * weights[0] // sum(weights)))
    least = 1 if total - largest >= amount - 1 else 0
    holding, rest = [largest] + [least] * (amount - 1), total - largest - least * (amount - 1)
    while rest > 0:
        movable = [i for i in range(1, amount) if holding[i] < largest] or [i for i in range(1, amount) if holding[i] < reach]
        mass, left = sum([weights[i] for i in movable]), rest
        for i in movable:
            addition = min(reach - holding[i], max(1, left * weights[i] // mass), rest)
            holding[i] = holding[i] + addition
            rest = rest - addition
    return np.array(holding)


def scatter_about(stream_key, dims, spread, bound, pieces=(), kind=jnp.bfloat16):
    array = spread * jax.random.normal(stream_key, dims, jnp.float32)
    if pieces:
        array = array * shard_levels(stream_key, dims, pieces, -0.22, 0.18)
    return jnp.clip(array, -bound, bound).astype(kind)


def setup_inputs(seed: int = 0, part: int = 0) -> dict:
    keys = jax.random.split(jax.random.key(seed), 12)
    own_keys = jax.random.split(jax.random.fold_in(keys[11], part), 12)
    tokens = scatter_about(own_keys[0], (TOKENS, D), 1.0, 6.0, ((0, 16),))
    routes_keys = jax.random.split(jax.random.fold_in(own_keys[1], 1), TOKENS // TOK_DEV)
    routes_turns = jax.random.permutation(jax.random.fold_in(own_keys[1], 3), TOKENS // TOK_DEV)
    routes = jax.vmap(lambda own, number: deal_out(jax.random.fold_in(own_keys[1], 2), own, number, TOK_DEV, EXPERTS, 1, CAP, 2))(routes_keys, routes_turns).reshape((TOKENS, 1))
    encoder = scatter_about(own_keys[2], (EXPERTS, LAT_EXP, D), D ** -0.5, 0.09375, ((0, 16),))
    encoder_bias = scatter_about(own_keys[3], (EXPERTS, LAT_EXP), 0.5, 3.0, ((0, 16),), jnp.float32)
    decoder = scatter_about(own_keys[4], (EXPERTS, LAT_EXP, D), LAT_EXP ** -0.5, 1.0, ((0, 16),))
    encoder_mean = scatter_about(own_keys[5], (EXPERTS, LAT_EXP, D), (D // (3 * LAT_EXP)), 256.0, ((0, 16),), jnp.float32)
    encoder_second = jnp.clip(jnp.exp(math.log(1638400) - 4.6051702 * jax.random.uniform(own_keys[6], (EXPERTS, LAT_EXP, D), jnp.float32) ** shard_levels(own_keys[6], (EXPERTS, LAT_EXP, D), ((0, 16),), -0.2, 0.2)), 16384.0, 1638400)
    bias_mean = scatter_about(own_keys[7], (EXPERTS, LAT_EXP), (D // (3 * LAT_EXP)), 256.0, ((0, 16),), jnp.float32)
    bias_second = jnp.clip(jnp.exp(math.log(1638400) - 4.6051702 * jax.random.uniform(own_keys[8], (EXPERTS, LAT_EXP), jnp.float32) ** shard_levels(own_keys[8], (EXPERTS, LAT_EXP), ((0, 16),), -0.2, 0.2)), 16384.0, 1638400)
    decoder_mean = scatter_about(own_keys[9], (EXPERTS, LAT_EXP, D), 3.0, 18.0, ((0, 16),), jnp.float32)
    decoder_second = jnp.clip(jnp.exp(math.log(400.0) - 4.6051702 * jax.random.uniform(own_keys[10], (EXPERTS, LAT_EXP, D), jnp.float32) ** shard_levels(own_keys[10], (EXPERTS, LAT_EXP, D), ((0, 16),), -0.2, 0.2)), 4.0, 400.0)
    return dict(tokens=tokens, routes=routes, encoder=encoder, encoder_bias=encoder_bias, decoder=decoder, encoder_mean=encoder_mean, encoder_second=encoder_second, bias_mean=bias_mean, bias_second=bias_second, decoder_mean=decoder_mean, decoder_second=decoder_second)


beta_first = 0.9
beta_second = 0.999
adam_eps = 1e-08
learn_rate = 0.001
sparsity = 4.0
step_count = 1000.0

def rounded(value):
    return lax.optimization_barrier(value.astype(jnp.bfloat16)).astype(jnp.float32)

def adam_update(param, grad, mean, second):
    mean_new = beta_first * mean + (1.0 - beta_first) * grad
    second_new = beta_second * second + (1.0 - beta_second) * grad * grad
    corr_first = 1.0 - beta_first ** step_count
    corr_second = 1.0 - beta_second ** step_count
    update = mean_new / corr_first / (jnp.sqrt(second_new / corr_second) + adam_eps)
    return (param.astype(jnp.float32) - learn_rate * update, mean_new, second_new)

def reference(tokens, routes, encoder, encoder_bias, decoder, encoder_mean, encoder_second, bias_mean, bias_second, decoder_mean, decoder_second):
    block_count = TOKENS // TOK_DEV
    token_blocks = tokens.reshape(block_count, TOK_DEV, D)
    route_blocks = routes[:, 0].astype(jnp.int32).reshape(block_count, TOK_DEV)

    def scan_step(totals, block_item):
        grad_enc, grad_dec, grad_bias = totals
        block_tokens, block_route = block_item
        enc_rows = encoder[block_route].astype(jnp.float32)
        dec_rows = decoder[block_route].astype(jnp.float32)
        tokens_wide = block_tokens.astype(jnp.float32)
        preact = jnp.einsum('td,tld->tl', tokens_wide, enc_rows) + encoder_bias[block_route]
        activity = rounded(jnp.maximum(preact, 0.0))
        rebuilt = jnp.einsum('tl,tld->td', activity, dec_rows)
        residue = rounded(rebuilt - tokens_wide)
        grad_activity = jnp.einsum('td,tld->tl', residue, dec_rows) + sparsity
        grad_preact = jnp.where(preact > 0.0, grad_activity, 0.0)
        grad_narrow = rounded(grad_preact)
        grad_dec = grad_dec.at[block_route].add(activity[:, :, None] * residue[:, None, :])
        grad_enc = grad_enc.at[block_route].add(grad_narrow[:, :, None] * tokens_wide[:, None, :])
        grad_bias = grad_bias.at[block_route].add(grad_preact)
        return ((grad_enc, grad_dec, grad_bias), rebuilt.astype(jnp.bfloat16))
    zeros_big = jnp.zeros((EXPERTS, LAT_EXP, D), jnp.float32)
    zeros_small = jnp.zeros((EXPERTS, LAT_EXP), jnp.float32)
    (grad_enc, grad_dec, grad_bias), rebuilt = lax.scan(scan_step, (zeros_big, zeros_big, zeros_small), (token_blocks, route_blocks))
    new_enc, enc_mean, enc_second = adam_update(encoder, grad_enc, encoder_mean, encoder_second)
    new_bias, new_bias_mean, new_bias_second = adam_update(encoder_bias, grad_bias, bias_mean, bias_second)
    new_dec, dec_mean, dec_second = adam_update(decoder, grad_dec, decoder_mean, decoder_second)
    return (new_enc.astype(jnp.bfloat16), new_bias, new_dec.astype(jnp.bfloat16), enc_mean, enc_second, new_bias_mean, new_bias_second, dec_mean, dec_second, rebuilt.reshape(TOKENS, D))
```

```python
import jax
import jax.numpy as jnp
from jax import lax
from jax.sharding import PartitionSpec as P

beta_first = 0.9
beta_second = 0.999
adam_eps = 1e-08
learn_rate = 0.001
sparsity = 4.0
step_count = 1000.0
empty_mark = 8.0
peer_axes = ("expert", "latent")


def adam_update(param, grad, mean, second):
    mean_new = beta_first * mean + (1.0 - beta_first) * grad
    second_new = beta_second * second + (1.0 - beta_second) * grad * grad
    corr_first = 1.0 - beta_first**step_count
    corr_second = 1.0 - beta_second**step_count
    update = mean_new / corr_first / (jnp.sqrt(second_new / corr_second) + adam_eps)
    return (param.astype(jnp.float32) - learn_rate * update, mean_new, second_new)


def dot(a, b, dims):
    return lax.dot_general(a, b, (dims, ((), ())), preferred_element_type=jnp.float32)


def body(
    tokens,
    routes,
    encoder,
    encoder_bias,
    decoder,
    encoder_mean,
    encoder_second,
    bias_mean,
    bias_second,
    decoder_mean,
    decoder_second,
):
    n_peers = lax.axis_size("expert") * lax.axis_size("latent")
    own, lat, width = encoder.shape
    experts_all = n_peers * own
    tok_rows = tokens.shape[0]
    capacity = 2 * tok_rows // experts_all
    slots = experts_all * capacity
    bf16, f32 = jnp.bfloat16, jnp.float32

    route = routes[:, 0]
    picked = route[:, None] == jnp.arange(experts_all, dtype=jnp.int32)[None, :]
    lower = jnp.arange(tok_rows)[:, None] > jnp.arange(tok_rows)[None, :]
    earlier = dot(lower.astype(bf16), picked.astype(bf16), ((1,), (0,)))
    rank = jnp.sum(jnp.where(picked, earlier, 0.0), axis=1).astype(jnp.int32)
    slot = route * capacity + rank
    place = jnp.arange(slots, dtype=jnp.int32)[:, None] == slot[None, :]
    place_bf = place.astype(bf16)
    vacant = ~jnp.any(place, axis=1)
    mark = jnp.where(
        vacant[:, None] & (jnp.arange(width)[None, :] == 0), empty_mark, 0.0
    )
    packed = (dot(place_bf, tokens, ((1,), (0,))) + mark).astype(bf16)
    rows = lax.all_to_all(
        packed.reshape(n_peers, own * capacity, width), peer_axes, 0, 0, tiled=True
    ).reshape(slots, width)

    valid = rows[:, 0:1] < empty_mark - 1.0
    row_expert = (jnp.arange(slots, dtype=jnp.int32) // capacity) % own
    latent_expert = jnp.arange(own * lat, dtype=jnp.int32) // lat
    allowed = (row_expert[:, None] == latent_expert[None, :]) & valid
    enc = encoder.reshape(own * lat, width)
    dec = decoder.reshape(own * lat, width)
    preact = dot(rows, enc, ((1,), (1,))) + encoder_bias.reshape(1, own * lat)
    active = (preact > 0.0) & allowed
    activity = jnp.where(active, preact, 0.0).astype(bf16)
    rebuilt = dot(activity, dec, ((1,), (0,)))
    outgoing = rebuilt.astype(bf16)
    back = lax.all_to_all(
        outgoing.reshape(n_peers, own * capacity, width), peer_axes, 0, 0, tiled=True
    ).reshape(slots, width)
    residue = (rebuilt - rows.astype(f32)).astype(bf16)
    grad_activity = dot(residue, dec, ((1,), (1,))) + sparsity
    grad_preact = jnp.where(active, grad_activity, 0.0)
    grad_bias = jnp.sum(grad_preact, axis=0).reshape(own, lat)
    grad_enc = dot(grad_preact.astype(bf16), rows, ((0,), (0,))).reshape(own, lat, width)
    grad_dec = dot(activity, residue, ((0,), (0,))).reshape(own, lat, width)
    new_enc, enc_mean, enc_second = adam_update(encoder, grad_enc, encoder_mean, encoder_second)
    new_bias, new_bias_mean, new_bias_second = adam_update(
        encoder_bias, grad_bias, bias_mean, bias_second
    )
    new_dec, dec_mean, dec_second = adam_update(decoder, grad_dec, decoder_mean, decoder_second)

    reconstruction = dot(place_bf, back, ((0,), (0,))).astype(bf16)
    return (
        new_enc.astype(bf16),
        new_bias,
        new_dec.astype(bf16),
        enc_mean,
        enc_second,
        new_bias_mean,
        new_bias_second,
        dec_mean,
        dec_second,
        reconstruction,
    )


def solution(mesh):
    rows = P(("groups", "expert", "latent"), None)
    cubes = P(("groups", "expert", "latent"), None, None)
    in_specs = (rows, rows, cubes, rows, cubes, cubes, cubes, rows, rows, cubes, cubes)
    out_specs = (cubes, rows, cubes, cubes, cubes, rows, rows, cubes, cubes, rows)
    return jax.shard_map(body, mesh=mesh, in_specs=in_specs, out_specs=out_specs, check_vma=False)
```

```python
import jax
import jax.numpy as jnp
from jax import lax
from jax.sharding import PartitionSpec as P

beta_first = 0.9
beta_second = 0.999
adam_eps = 1e-08
learn_rate = 0.001
sparsity = 4.0
step_count = 1000.0
peer_axes = ("expert", "latent")


def adam_update(param, grad, mean, second):
    mean_new = beta_first * mean + (1.0 - beta_first) * grad
    second_new = beta_second * second + (1.0 - beta_second) * grad * grad
    corr_first = 1.0 - beta_first**step_count
    corr_second = 1.0 - beta_second**step_count
    update = mean_new / corr_first / (jnp.sqrt(second_new / corr_second) + adam_eps)
    return (param.astype(jnp.float32) - learn_rate * update, mean_new, second_new)


def dot(a, b, dims):
    return lax.dot_general(a, b, (dims, ((), ())), preferred_element_type=jnp.float32)


def body(
    tokens,
    routes,
    encoder,
    encoder_bias,
    decoder,
    encoder_mean,
    encoder_second,
    bias_mean,
    bias_second,
    decoder_mean,
    decoder_second,
):
    all_axes = ("groups",) + peer_axes
    n_groups, n_cores = lax.axis_size("groups"), lax.axis_size("latent")
    n_peers = lax.axis_size("expert") * n_cores
    n_chips = n_peers // n_cores
    own, lat, width = encoder.shape
    tok_rows = tokens.shape[0]
    chip_experts = n_cores * own
    half = own * lat
    block_full = 2 * tok_rows // n_peers
    block_small = 3 * block_full // 4
    bf16, f32, i32 = jnp.bfloat16, jnp.float32, jnp.int32
    core = lax.axis_index("latent")
    chip = lax.axis_index("expert")
    swap = [(i, n_cores - 1 - i) for i in range(n_cores)]

    route = routes[:, 0]
    everyone = lax.all_to_all(
        jnp.broadcast_to(route[None, :], (n_groups * n_peers, tok_rows)),
        all_axes,
        0,
        0,
        tiled=True,
    )
    enc_mine, dec_mine = encoder.reshape(half, width), decoder.reshape(half, width)
    enc_other = lax.ppermute(enc_mine, "latent", swap)
    dec_other = lax.ppermute(dec_mine, "latent", swap)
    bias_mine = encoder_bias.reshape(1, half)
    bias_other = lax.ppermute(bias_mine, "latent", swap)

    order = jnp.arange(tok_rows, dtype=i32)
    before = (order[:, None] < order[None, :]).astype(bf16)
    loads = jnp.sum(
        (everyone[:, :, None] // chip_experts == jnp.arange(n_chips)).astype(i32), axis=1
    )
    fits = jnp.max(loads) <= n_cores * block_small

    to_chip = route[None, :] // chip_experts == jnp.arange(n_chips, dtype=i32)[:, None]
    turn = jnp.sum(
        jnp.where(to_chip, dot(to_chip.astype(bf16), before, ((1,), (0,))), 0.0), axis=0
    ).astype(i32)
    target = route // chip_experts * n_cores + turn % n_cores
    spot = turn // n_cores

    peers = lax.dynamic_slice_in_dim(
        everyone, lax.axis_index("groups") * n_peers, n_peers, axis=0
    )
    for_chip = peers // chip_experts == chip
    peer_turn = dot(for_chip.astype(bf16), before, ((1,), (0,))).astype(i32)
    for_me = for_chip & (peer_turn % n_cores == core)
    inside = peers % chip_experts
    local = (inside // own + n_cores - core) % n_cores * own + inside % own
    label = jnp.where(for_me, local + 1, 0)
    peer_spot = peer_turn // n_cores

    def step(block):
        slots = n_peers * block
        place = jnp.arange(slots, dtype=i32)[:, None] == (target * block + spot)[None, :]
        place = place.astype(bf16)
        packed = dot(place, tokens, ((1,), (0,))).astype(bf16)
        rows = lax.all_to_all(
            packed.reshape(n_peers, block, width), peer_axes, 0, 0, tiled=True
        ).reshape(slots, width)
        hit = peer_spot[:, None, :] == jnp.arange(block, dtype=i32)[None, :, None]
        row_label = jnp.sum(jnp.where(hit, label[:, None, :], 0), axis=2).reshape(slots, 1)
        ahead = jnp.arange(half, dtype=i32)[None, :] // lat + 1
        allow_mine, allow_other = row_label == ahead, row_label == ahead + own

        def encode(enc, bias, allowed):
            preact = dot(rows, enc, ((1,), (1,))) + bias
            active = (preact > 0.0) & allowed
            return active, jnp.where(active, preact, 0.0).astype(bf16)

        active_mine, act_mine = encode(enc_mine, bias_mine, allow_mine)
        active_other, act_other = encode(enc_other, bias_other, allow_other)
        rebuilt = dot(
            jnp.concatenate([act_mine, act_other], axis=1),
            jnp.concatenate([dec_mine, dec_other], axis=0),
            ((1,), (0,)),
        )
        outgoing = rebuilt.astype(bf16)
        back = lax.all_to_all(
            outgoing.reshape(n_peers, block, width), peer_axes, 0, 0, tiled=True
        ).reshape(slots, width)
        residue = (rebuilt - rows.astype(f32)).astype(bf16)

        def gradients(active, act, dec):
            grad_activity = dot(residue, dec, ((1,), (1,))) + sparsity
            grad_preact = jnp.where(active, grad_activity, 0.0)
            return (
                dot(grad_preact.astype(bf16), rows, ((0,), (0,))),
                dot(act, residue, ((0,), (0,))),
                jnp.sum(grad_preact, axis=0, keepdims=True),
            )

        away = gradients(active_other, act_other, dec_other)
        arrived = [lax.ppermute(g, "latent", swap) for g in away]
        here = gradients(active_mine, act_mine, dec_mine)
        grad_enc, grad_dec, grad_bias = [x + y for x, y in zip(here, arrived)]
        new_enc, enc_mean, enc_second = adam_update(
            encoder, grad_enc.reshape(encoder.shape), encoder_mean, encoder_second
        )
        new_bias, new_bias_mean, new_bias_second = adam_update(
            encoder_bias, grad_bias.reshape(own, lat), bias_mean, bias_second
        )
        new_dec, dec_mean, dec_second = adam_update(
            decoder, grad_dec.reshape(decoder.shape), decoder_mean, decoder_second
        )
        reconstruction = dot(place, back, ((0,), (0,))).astype(bf16)
        return (
            new_enc.astype(bf16),
            new_bias,
            new_dec.astype(bf16),
            enc_mean,
            enc_second,
            new_bias_mean,
            new_bias_second,
            dec_mean,
            dec_second,
            reconstruction,
        )

    return lax.cond(fits, lambda: step(block_small), lambda: step(block_full))


def solution(mesh):
    rows = P(("groups", "expert", "latent"), None)
    cubes = P(("groups", "expert", "latent"), None, None)
    in_specs = (rows, rows, cubes, rows, cubes, cubes, cubes, rows, rows, cubes, cubes)
    out_specs = (cubes, rows, cubes, cubes, cubes, rows, rows, cubes, cubes, rows)
    return jax.shard_map(body, mesh=mesh, in_specs=in_specs, out_specs=out_specs, check_vma=False)
```

```python
import jax
import jax.numpy as jnp
from jax import lax
from jax.sharding import PartitionSpec as P

beta_first = 0.9
beta_second = 0.999
adam_eps = 1e-08
learn_rate = 0.001
sparsity = 4.0
step_count = 1000.0
peer_axes = ("expert", "latent")


def adam_update(param, grad, mean, second):
    mean_new = beta_first * mean + (1.0 - beta_first) * grad
    second_new = beta_second * second + (1.0 - beta_second) * grad * grad
    corr_first = 1.0 - beta_first**step_count
    corr_second = 1.0 - beta_second**step_count
    update = mean_new / corr_first / (jnp.sqrt(second_new / corr_second) + adam_eps)
    return (param.astype(jnp.float32) - learn_rate * update, mean_new, second_new)


def dot(a, b, dims):
    return lax.dot_general(a, b, (dims, ((), ())), preferred_element_type=jnp.float32)


def body(
    tokens,
    routes,
    encoder,
    encoder_bias,
    decoder,
    encoder_mean,
    encoder_second,
    bias_mean,
    bias_second,
    decoder_mean,
    decoder_second,
):
    all_axes = ("groups",) + peer_axes
    n_groups, n_cores = lax.axis_size("groups"), lax.axis_size("latent")
    n_peers = lax.axis_size("expert") * n_cores
    n_chips = n_peers // n_cores
    own, lat, width = encoder.shape
    tok_rows = tokens.shape[0]
    chip_experts = n_cores * own
    half = own * lat
    block_full = 2 * tok_rows // n_peers
    block_small = 3 * block_full // 4
    bf16, f32, i32 = jnp.bfloat16, jnp.float32, jnp.int32
    core = lax.axis_index("latent")
    chip = lax.axis_index("expert")
    swap = [(i, n_cores - 1 - i) for i in range(n_cores)]

    route = routes[:, 0]
    everyone = lax.all_to_all(
        jnp.broadcast_to(route[None, :], (n_groups * n_peers, tok_rows)),
        all_axes,
        0,
        0,
        tiled=True,
    )
    enc_mine, dec_mine = encoder.reshape(half, width), decoder.reshape(half, width)
    enc_other = lax.ppermute(enc_mine, "latent", swap)
    dec_other = lax.ppermute(dec_mine, "latent", swap)
    bias_mine = encoder_bias.reshape(1, half)
    bias_other = lax.ppermute(bias_mine, "latent", swap)

    order = jnp.arange(tok_rows, dtype=i32)
    before = (order[:, None] < order[None, :]).astype(bf16)
    loads = jnp.sum(
        (everyone[:, :, None] // chip_experts == jnp.arange(n_chips)).astype(i32), axis=1
    )
    fits = jnp.max(loads) <= n_cores * block_small

    to_chip = route[None, :] // chip_experts == jnp.arange(n_chips, dtype=i32)[:, None]
    turn = jnp.sum(
        jnp.where(to_chip, dot(to_chip.astype(bf16), before, ((1,), (0,))), 0.0), axis=0
    ).astype(i32)
    target = route // chip_experts * n_cores + turn % n_cores
    spot = turn // n_cores

    peers = lax.dynamic_slice_in_dim(
        everyone, lax.axis_index("groups") * n_peers, n_peers, axis=0
    )
    for_chip = peers // chip_experts == chip
    peer_turn = dot(for_chip.astype(bf16), before, ((1,), (0,))).astype(i32)
    for_me = for_chip & (peer_turn % n_cores == core)
    inside = peers % chip_experts
    local = (inside // own + n_cores - core) % n_cores * own + inside % own
    label = jnp.where(for_me, local + 1, 0)
    peer_spot = peer_turn // n_cores

    def pack(block):
        at = jnp.where(spot < block, target * block + spot, -1)
        place = jnp.arange(n_peers * block, dtype=i32)[:, None] == at[None, :]
        place = place.astype(bf16)
        return place, dot(place, tokens, ((1,), (0,))).astype(bf16)

    def step(block, place, packed):
        slots = n_peers * block
        rows = lax.all_to_all(
            packed.reshape(n_peers, block, width), peer_axes, 0, 0, tiled=True
        ).reshape(slots, width)
        hit = peer_spot[:, None, :] == jnp.arange(block, dtype=i32)[None, :, None]
        row_label = jnp.sum(jnp.where(hit, label[:, None, :], 0), axis=2).reshape(slots, 1)
        ahead = jnp.arange(half, dtype=i32)[None, :] // lat + 1
        allow_mine, allow_other = row_label == ahead, row_label == ahead + own

        def encode(enc, bias, allowed):
            preact = dot(rows, enc, ((1,), (1,))) + bias
            active = (preact > 0.0) & allowed
            return active, jnp.where(active, preact, 0.0).astype(bf16)

        active_mine, act_mine = encode(enc_mine, bias_mine, allow_mine)
        active_other, act_other = encode(enc_other, bias_other, allow_other)
        rebuilt = dot(
            jnp.concatenate([act_mine, act_other], axis=1),
            jnp.concatenate([dec_mine, dec_other], axis=0),
            ((1,), (0,)),
        )
        outgoing = rebuilt.astype(bf16)
        back = lax.all_to_all(
            outgoing.reshape(n_peers, block, width), peer_axes, 0, 0, tiled=True
        ).reshape(slots, width)
        residue = (rebuilt - rows.astype(f32)).astype(bf16)

        def gradients(active, act, dec):
            grad_activity = dot(residue, dec, ((1,), (1,))) + sparsity
            grad_preact = jnp.where(active, grad_activity, 0.0)
            return (
                dot(grad_preact.astype(bf16), rows, ((0,), (0,))),
                dot(act, residue, ((0,), (0,))),
                jnp.sum(grad_preact, axis=0, keepdims=True),
            )

        away = gradients(active_other, act_other, dec_other)
        arrived = [lax.ppermute(g, "latent", swap) for g in away]
        here = gradients(active_mine, act_mine, dec_mine)
        grad_enc, grad_dec, grad_bias = [x + y for x, y in zip(here, arrived)]
        new_enc, enc_mean, enc_second = adam_update(
            encoder, grad_enc.reshape(encoder.shape), encoder_mean, encoder_second
        )
        new_bias, new_bias_mean, new_bias_second = adam_update(
            encoder_bias, grad_bias.reshape(own, lat), bias_mean, bias_second
        )
        new_dec, dec_mean, dec_second = adam_update(
            decoder, grad_dec.reshape(decoder.shape), decoder_mean, decoder_second
        )
        reconstruction = dot(place, back, ((0,), (0,))).astype(bf16)
        return (
            new_enc.astype(bf16),
            new_bias,
            new_dec.astype(bf16),
            enc_mean,
            enc_second,
            new_bias_mean,
            new_bias_second,
            dec_mean,
            dec_second,
            reconstruction,
        )

    early = pack(block_small)
    return lax.cond(
        fits, lambda: step(block_small, *early), lambda: step(block_full, *pack(block_full))
    )


def solution(mesh):
    rows = P(("groups", "expert", "latent"), None)
    cubes = P(("groups", "expert", "latent"), None, None)
    in_specs = (rows, rows, cubes, rows, cubes, cubes, cubes, rows, rows, cubes, cubes)
    out_specs = (cubes, rows, cubes, cubes, cubes, rows, rows, cubes, cubes, rows)
    return jax.shard_map(body, mesh=mesh, in_specs=in_specs, out_specs=out_specs, check_vma=False)
```
